256 devices in a mesh: seq: 32 (over y, z), kvh: 8 (over x, core).
Axes of the slice: x: 4, y: 4, z: 8, core: 2. Of those that a mesh axis runs over, the one named last changes fastest.
Arguments:
- inputs: bfloat16 [32, 16384], P('kvh', 'seq'), may hold values from -6 to 6
- w_query: bfloat16 [16384, 16384], P('seq', 'kvh'), may hold values from -0.046875 to 0.046875
- w_key: bfloat16 [16384, 1024], P('seq', 'kvh'), may hold values from -0.125 to 0.125
- w_value: bfloat16 [16384, 1024], P('seq', 'kvh'), may hold values from -0.046875 to 0.046875
- w_output: bfloat16 [16384, 16384], P('kvh', 'seq'), may hold values from -0.046875 to 0.046875
- key_cache: bfloat16 [32, 16384, 8, 128], P(None, 'seq', 'kvh'), may hold values from -400 to 400
- value_cache: bfloat16 [32, 16384, 8, 128], P(None, 'seq', 'kvh'), may hold values from -6 to 6
- lengths: int32 [32], replicated, may hold values from 1 to 16384, 262144 in all
- positions: int32 [32], replicated, may hold values from 16384 to 32767
Outputs:
- attended: bfloat16 [32, 16384], P('kvh', 'seq')
The draws below stay inside these ranges and needn't reach their ends.
All inputs are finite; a program needn't handle non-finite values.
Results may differ from the reference program's by a relative error of at most 0.029.
Values may be sent and summed in bfloat16 or wider, within the bound.
A program may use at most 128 MiB of HBM per device.

```python
import math
import jax
import jax.numpy as jnp
import numpy as np
from jax import lax

D = 16384
QH = 128
KVH = 8
HD = 128
CTX_DEV = 512
ROWS = 32
CTX = 16384


def draw_key_cache(key, part):
    key = jax.random.fold_in(key, 11)
    base_key = jax.random.fold_in(key, 0)
    base = jax.random.normal(base_key, (ROWS, CTX, KVH, HD), jnp.float32) * 2.0
    return jnp.clip(base, -16.0, 16.0).astype(jnp.bfloat16)


def plant(values, own_key, smallest, largest):
    spot = [jax.random.randint(jax.random.fold_in(own_key, axis), (), 0, length) for axis, length in enumerate(values.shape)]
    longest = values.shape.index(max(values.shape))
    neighbour = spot[:longest] + [(spot[longest] + 1) % values.shape[longest]] + spot[longest + 1:]
    return values.at[tuple(spot)].set(smallest).at[tuple(neighbour)].set(largest)


def block_levels(rng, dims, shards, least, largest):
    loudness = 1.0
    for dim, shards_of in shards:
        draws = jax.random.uniform(jax.random.fold_in(jax.random.fold_in(rng, 6), dim), (shards_of,), jnp.float32, least / len(shards), largest / len(shards))
        loudness = loudness * jnp.repeat(jnp.exp(draws), dims[dim] // shards_of).reshape((-1,) + (1,) * (len(dims) - 1 - dim))
    return loudness


def profile(count, total, limit, slope):
    loads = [(1 << 20) // math.isqrt(standing ** slope) + 1 for standing in range(2, count + 1)]
    surplus, counts = total - limit - (count - 1), [1] * (count - 1)
    while surplus > 0:
        candidates = [i for i in range(count - 1) if counts[i] < limit]
        pool, left = sum([loads[i] for i in candidates]), surplus
        for i in candidates:
            more = min(limit - counts[i], max(1, left * loads[i] // pool), surplus)
            counts[i] = counts[i] + more
            surplus = surplus - more
    return np.array([limit] + counts)


def ragged(own_key, count, total, most, slope):
    if count == 2:
        one = jax.random.randint(own_key, (), max(1, total - most), min(most, total - 1) + 1)
        return jnp.stack([one, total - one])
    sizes = jnp.asarray(profile(count, total, most, slope), jnp.int32)
    pairs = (count - 1) // 2
    giver, receiver = sizes[1:1 + 2 * pairs:2], sizes[2:2 + 2 * pairs:2]
    room = jnp.minimum(giver - 1, most - receiver)
    moved = jax.random.randint(jax.random.fold_in(own_key, 1), (pairs,), 0, 1 << 20) % (room + 1)
    sizes = sizes.at[1:1 + 2 * pairs:2].set(giver - moved).at[2:2 + 2 * pairs:2].set(receiver + moved)
    return sizes[jax.random.permutation(jax.random.fold_in(own_key, 2), count)]


def gaussian(own_key, dims, spread, limit, pieces=(), held_as=jnp.bfloat16):
    drawn = spread * jax.random.normal(own_key, dims, jnp.float32)
    if pieces:
        drawn = drawn * block_levels(own_key, dims, pieces, -0.22, 0.18)
    return jnp.clip(drawn, -limit, limit).astype(held_as)


def setup_inputs(seed: int = 0) -> dict:
    streams_of = jax.random.split(jax.random.key(seed), 10)
    return {
        "inputs": gaussian(streams_of[0], (ROWS, D), 1.0, 6.0, ((0, 8), (1, 32))),
        "w_query": gaussian(streams_of[1], (D, QH * HD), D ** -0.5, 0.046875, ((0, 32), (1, 8))),
        "w_key": gaussian(streams_of[2], (D, KVH * HD), (D // 9) ** -0.5, 0.125, ((0, 32), (1, 8))),
        "w_value": gaussian(streams_of[3], (D, KVH * HD), D ** -0.5, 0.046875, ((0, 32), (1, 8))),
        "w_output": gaussian(streams_of[4], (QH * HD, D), (QH * HD) ** -0.5, 0.046875, ((0, 8), (1, 32))),
        "key_cache": draw_key_cache(jax.random.fold_in(streams_of[9], 71), 0),
        "value_cache": gaussian(streams_of[6], (ROWS, CTX, KVH, HD), 1.0, 6.0, ((1, 32), (2, 8))),
        "lengths": ragged(streams_of[7], ROWS, ROWS * CTX // 2, CTX, 2).astype(jnp.int32),
        "positions": plant(jax.random.randint(streams_of[8], (ROWS,), CTX, 2 * CTX), jax.random.fold_in(streams_of[8], 1), CTX, (2 * CTX) - 1).astype(jnp.int32),
    }


def apply_rotary(tensor, position):
    half = tensor.shape[-1] // 2
    freq = 500000.0 ** (-(jnp.arange(half, dtype=jnp.float32) * 2.0 / tensor.shape[-1]))
    angle = position.astype(jnp.float32)[:, None, None] * freq[None, None, :]
    cosine = jnp.cos(angle)
    sine = jnp.sin(angle)
    first = tensor[..., :half]
    second = tensor[..., half:]
    return jnp.concatenate([first * cosine - second * sine, second * cosine + first * sine], axis=-1)


def reference(inputs, w_query, w_key, w_value, w_output, key_cache, value_cache, lengths, positions):
    group = QH // KVH
    blocks = CTX // CTX_DEV
    scale = HD ** -0.5
    query_full = jnp.dot(inputs, w_query, preferred_element_type=jnp.float32).reshape(ROWS, QH, HD)
    key_full = jnp.dot(inputs, w_key, preferred_element_type=jnp.float32).reshape(ROWS, KVH, HD)
    value_full = jnp.dot(inputs, w_value, preferred_element_type=jnp.float32).reshape(ROWS, KVH, HD)
    queries = apply_rotary(query_full, positions).astype(jnp.bfloat16).reshape(ROWS, KVH, group, HD)
    keys_new = apply_rotary(key_full, positions).astype(jnp.bfloat16)
    values_new = value_full.astype(jnp.bfloat16)
    new_score = jnp.einsum("rgqd,rgd->rgq", queries.astype(jnp.float32), keys_new.astype(jnp.float32)) * scale

    def one_row(items):
        query_row, key_row, value_row, length_row, score_row, value_new_row = items
        key_blocks = key_row.astype(jnp.float32).reshape(blocks, CTX_DEV, KVH, HD)
        value_blocks = value_row.astype(jnp.float32).reshape(blocks, CTX_DEV, KVH, HD)
        scores = jnp.einsum("gqd,bcgd->bgqc", query_row.astype(jnp.float32), key_blocks) * scale
        valid = (jnp.arange(CTX, dtype=jnp.int32).reshape(blocks, CTX_DEV) < length_row)[:, None, None, :]
        masked = jnp.where(valid, scores, jnp.float32(-1e30))
        block_max = jnp.max(masked, axis=-1)
        weights = jnp.where(valid, jnp.exp(masked - block_max[..., None]), jnp.float32(0.0))
        block_total = jnp.sum(weights, axis=-1)
        rounded = weights.astype(jnp.bfloat16).astype(jnp.float32)
        block_sum = jnp.einsum("bgqc,bcgd->bgqd", rounded, value_blocks)
        top = jnp.maximum(jnp.max(block_max, axis=0), score_row)
        factor = jnp.exp(block_max - top[None])
        own = jnp.exp(score_row - top)
        total = own + jnp.sum(factor * block_total, axis=0)
        summed = own[..., None] * value_new_row.astype(jnp.float32)[:, None, :] + jnp.sum(factor[..., None] * block_sum, axis=0)
        return (summed / total[..., None]).astype(jnp.bfloat16).reshape(QH * HD)

    heads_out = lax.map(one_row, (queries, key_cache, value_cache, lengths, new_score, values_new))
    return jnp.dot(heads_out, w_output, preferred_element_type=jnp.float32).astype(jnp.bfloat16)
```

```python
import jax
import jax.numpy as jnp
import numpy as np
from jax import lax
from jax.experimental import pallas as pl
from jax.experimental.pallas import tpu as pltpu
from jax.sharding import PartitionSpec as P

QH = 128
KVH = 8
HD = 128
GROUP = QH // KVH
MESH = pl.DeviceIdType.MESH
F32 = jnp.float32
BF16 = jnp.bfloat16
ROWS_STEP = 8


def rotary_table():
    half = HD // 2
    freq = 500000.0 ** (-np.arange(half, dtype=np.float64) * 2.0 / HD)
    return np.tile(freq.astype(np.float32), 2).reshape(1, HD)


def by_distance(sizes):
    offsets = list(np.ndindex(*sizes))
    return sorted(offsets, key=lambda o: sum(min(d, n - d) for d, n in zip(o, sizes)))


SEQ_SIZES = (4, 8)
KVH_SIZES = (4, 2)
SEQ_OFFSETS = by_distance(SEQ_SIZES)
KVH_OFFSETS = by_distance(KVH_SIZES)


def peer(index, offset, sizes):
    outer, inner = sizes
    return ((index // inner + offset[0]) % outer) * inner + (index % inner + offset[1]) % inner


def kernel(
    lengths_hbm, positions_hbm, freq_hbm, inputs, wq_hbm, wk_hbm, wv_hbm, wo_hbm, key_hbm, value_hbm,
    out_ref,
    lengths, positions, freq, x_own, wq, wk, wv, wo, keys, values,
    x_all, rel, q_send, q_recv, stat_send, stat_recv, q_all, q_block,
    part_send, part_recv, heads_all, out_send, out_recv,
    load_sem, send_sem, recv_sem, group_sem,
):
    seq = lax.axis_index("seq")
    kvh = lax.axis_index("kvh")
    n_seq = len(SEQ_OFFSETS)
    n_kvh = len(KVH_OFFSETS)
    rows = q_all.shape[0]
    share = x_own.shape[0]
    block = keys.shape[1]
    scale = HD ** (-0.5)
    lanes = ROWS_STEP * GROUP
    seq_peers = [peer(seq, o, SEQ_SIZES) for o in SEQ_OFFSETS]
    kvh_peers = [peer(kvh, o, KVH_SIZES) for o in KVH_OFFSETS]
    place_of = {o: p for p, o in enumerate(SEQ_OFFSETS)}
    back = [place_of[tuple(-d % n for d, n in zip(o, SEQ_SIZES))] for o in SEQ_OFFSETS]
    far_first = list(range(n_seq - 1, 0, -1))

    def load(src, dst, n):
        copy = pltpu.make_async_copy(src, dst, load_sem.at[n])
        copy.start()
        return copy

    x_load = load(inputs, x_own, 0)
    small = [load(positions_hbm, positions, 1), load(freq_hbm, freq, 2), load(lengths_hbm, lengths, 3)]
    wk_load = load(wk_hbm, wk, 4)
    wv_load = load(wv_hbm, wv, 5)
    wq_load = load(wq_hbm, wq, 6)
    key_load = load(key_hbm, keys, 7)
    value_load = load(value_hbm, values, 8)
    wo_load = load(wo_hbm, wo, 9)

    barrier = pltpu.get_barrier_semaphore()
    for p in far_first:
        pl.semaphore_signal(barrier, inc=1, device_id={"seq": seq_peers[p]}, device_id_type=MESH)
    for p in range(n_kvh - 1, 0, -1):
        pl.semaphore_signal(barrier, inc=1, device_id={"kvh": kvh_peers[p]}, device_id_type=MESH)
    q_block[...] = jnp.zeros_like(q_block)
    x_load.wait()
    x_all[kvh] = x_own[...].astype(F32)
    pl.semaphore_wait(barrier, n_seq + n_kvh - 2)

    def send(axis, to, src, dst, phase, arrived):
        pltpu.make_async_remote_copy(
            src_ref=src, dst_ref=dst, send_sem=send_sem.at[phase], recv_sem=arrived,
            device_id={axis: to}, device_id_type=MESH,
        ).start()

    def sums_of(ref, count, phase, arrived):
        return pltpu.make_async_remote_copy(
            src_ref=ref.at[pl.ds(0, count)], dst_ref=ref.at[pl.ds(0, count)],
            send_sem=send_sem.at[phase], recv_sem=arrived,
            device_id={"kvh": kvh_peers[1]}, device_id_type=MESH,
        )

    def received(ref, count, phase):
        sums_of(ref, count, phase, recv_sem.at[phase]).wait_recv()

    def sent(ref, count, phase):
        sums_of(ref, count, phase, recv_sem.at[phase]).wait_send()

    for p in range(n_kvh - 1, 0, -1):
        send("kvh", kvh_peers[p], x_all.at[kvh], x_all.at[kvh], 0, recv_sem.at[0])

    for copy in small:
        copy.wait()
    angle = positions[seq].astype(F32) * freq[...]
    cosine = jnp.cos(angle)
    sine = jnp.sin(angle)
    lane = lax.broadcasted_iota(jnp.int32, (1, HD), 1)
    sine = jnp.where(lane < HD // 2, -sine, sine)

    def rotate(t):
        return t * cosine + pltpu.roll(t, HD // 2, 1) * sine

    wk_load.wait()
    wv_load.wait()
    wq_load.wait()
    received(x_all, n_kvh - 1, 0)
    x = jnp.concatenate([x_all[i] for i in range(n_kvh)], axis=0).astype(BF16)

    for c in range(0, GROUP, 2):
        part = jnp.dot(x, wq[:, c * HD : (c + 2) * HD], preferred_element_type=F32)
        rel[pl.ds(c, rows, stride=GROUP), :] = part[:, :HD]
        rel[pl.ds(c + 1, rows, stride=GROUP), :] = part[:, HD:]
    q_send[...] = rel[...].astype(BF16).reshape(q_send.shape)

    for p in far_first:
        to = seq_peers[p]
        send("seq", to, q_send.at[to], q_recv.at[seq], 1, recv_sem.at[1])
    q_recv[seq] = q_send[seq]
    k_part = jnp.dot(x, wk[...], preferred_element_type=F32)
    v_part = jnp.dot(x, wv[...], preferred_element_type=F32)
    for r in range(rows):
        stat_send[r, 2:3, :] = k_part[r : r + 1, :]
        stat_send[r, 3:4, :] = v_part[r : r + 1, :]
    received(q_recv, n_seq - 1, 1)
    q_own = rotate(jnp.sum(q_recv[...].astype(F32), axis=0)).astype(BF16)
    q_all[seq] = q_own

    for p in far_first:
        send("seq", seq_peers[p], q_all.at[seq], q_all.at[seq], 2, group_sem.at[back[p] // ROWS_STEP])
    sent(x_all, n_kvh - 1, 0)
    sent(q_send, n_seq - 1, 1)

    place = seq * block + lax.broadcasted_iota(jnp.int32, (block, lanes), 0)
    lane_row = lax.broadcasted_iota(jnp.int32, (1, lanes), 1) // GROUP
    key_load.wait()
    value_load.wait()
    for g in range(rows // ROWS_STEP):
        here = seq_peers[g * ROWS_STEP : (g + 1) * ROWS_STEP]
        sums_of(q_all, ROWS_STEP - (g == 0), 2, group_sem.at[g]).wait_recv()
        length = jnp.zeros((1, lanes), jnp.int32)
        for j, row in enumerate(here):
            q_block[j * GROUP : (j + 1) * GROUP, j * HD : (j + 1) * HD] = q_all[row]
            length = jnp.where(lane_row == j, lengths[row], length)
        k_cat = jnp.concatenate([keys[row] for row in here], axis=1)
        scores = (
            lax.dot_general(
                k_cat, q_block[...], (((1,), (1,)), ((), ())), preferred_element_type=F32
            )
            * scale
        )
        valid = place < length
        masked = jnp.where(valid, scores, F32(-1e30))
        block_max = jnp.max(masked, axis=0, keepdims=True)
        weights = jnp.where(valid, jnp.exp(masked - block_max), F32(0.0))
        total = jnp.sum(weights, axis=0, keepdims=True)
        turned = weights.T.astype(BF16)
        for j in range(0, ROWS_STEP, 2):
            v_cat = jnp.concatenate([values[here[j]], values[here[j + 1]]], axis=1)
            got = jnp.dot(
                turned[j * GROUP : (j + 2) * GROUP], v_cat, preferred_element_type=F32
            ).astype(BF16)
            part_send[here[j]] = got[:GROUP, :HD]
            part_send[here[j + 1]] = got[GROUP:, HD:]
        stats = jnp.concatenate([block_max, total], axis=0)
        for j, row in enumerate(here):
            stat_send[row, 0:2, :] = pltpu.roll(stats, (lanes - j * GROUP) % lanes, 1)
        for p in range((g + 1) * ROWS_STEP - 1, max(g * ROWS_STEP, 1) - 1, -1):
            to = seq_peers[p]
            send("seq", to, part_send.at[to], part_recv.at[seq], 3, recv_sem.at[3])
            send("seq", to, stat_send.at[to], stat_recv.at[seq], 4, recv_sem.at[4])

    part_recv[seq] = part_send[seq]
    stat_recv[seq] = stat_send[seq]
    sent(q_all, n_seq - 1, 2)
    received(stat_recv, n_seq - 1, 4)
    stats = stat_recv[...]
    k_new = rotate(jnp.sum(stats[:, 2, :], axis=0, keepdims=True)).astype(BF16).astype(F32)
    v_new = jnp.sum(stats[:, 3, :], axis=0, keepdims=True).astype(BF16).astype(F32)
    new_score = jnp.sum(q_own.astype(F32) * k_new, axis=1, keepdims=True) * scale
    maxima = stats[:, 0, :].T[:GROUP]
    totals = stats[:, 1, :].T[:GROUP]
    top = jnp.maximum(jnp.max(maxima, axis=1, keepdims=True), new_score)
    factor = jnp.exp(maxima - top)
    own = jnp.exp(new_score - top)
    total = jnp.sum(factor * totals, axis=1, keepdims=True) + own
    summed = own * v_new
    received(part_recv, n_seq - 1, 3)
    for s in range(rows):
        summed = summed + factor[:, s : s + 1] * part_recv[s].astype(F32)
    heads_all[seq] = (summed / total).astype(BF16)

    for p in far_first:
        send("seq", seq_peers[p], heads_all.at[seq], heads_all.at[seq], 5, recv_sem.at[5])
    sent(part_send, n_seq - 1, 3)
    sent(stat_send, n_seq - 1, 4)
    wo_load.wait()
    received(heads_all, n_seq - 1, 5)
    rel[...] = heads_all[...].reshape(rel.shape).astype(F32)
    heads = jnp.concatenate(
        [rel[pl.ds(h, rows, stride=GROUP), :].astype(BF16) for h in range(GROUP)], axis=1
    )
    terms = jnp.dot(heads, wo[...], preferred_element_type=F32)
    for i in range(rows // share):
        out_send[i] = terms[i * share : (i + 1) * share, :]

    for p in range(n_kvh - 1, 0, -1):
        to = kvh_peers[p]
        send("kvh", to, out_send.at[to], out_recv.at[kvh], 6, recv_sem.at[6])
    out_recv[kvh] = out_send[kvh]
    sent(heads_all, n_seq - 1, 5)
    received(out_recv, n_kvh - 1, 6)
    out_ref[...] = jnp.sum(out_recv[...], axis=0).astype(out_ref.dtype)
    sent(out_send, n_kvh - 1, 6)


def body(inputs, w_query, w_key, w_value, w_output, key_cache, value_cache, lengths, positions):
    n_kvh = lax.axis_size("kvh")
    share, depth = inputs.shape
    rows, block = key_cache.shape[:2]
    out_cols = w_output.shape[1]
    keys = jnp.transpose(key_cache, (0, 2, 1, 3)).reshape(rows, block, HD)
    values = jnp.transpose(value_cache, (0, 2, 1, 3)).reshape(rows, block, HD)
    vmem = pl.BlockSpec(memory_space=pltpu.VMEM)
    hbm = pl.BlockSpec(memory_space=pltpu.HBM)
    dma = pltpu.SemaphoreType.DMA
    return pl.pallas_call(
        kernel,
        out_shape=jax.ShapeDtypeStruct((share, out_cols), BF16),
        in_specs=[hbm] * 10,
        out_specs=vmem,
        scratch_shapes=[
            pltpu.SMEM(lengths.shape, jnp.int32),
            pltpu.SMEM(positions.shape, jnp.int32),
            pltpu.VMEM((1, HD), F32),
            pltpu.VMEM((share, depth), BF16),
            pltpu.VMEM(w_query.shape, BF16),
            pltpu.VMEM(w_key.shape, BF16),
            pltpu.VMEM(w_value.shape, BF16),
            pltpu.VMEM(w_output.shape, BF16),
            pltpu.VMEM(keys.shape, BF16),
            pltpu.VMEM(values.shape, BF16),
            pltpu.VMEM((n_kvh, share, depth), F32),
            pltpu.VMEM((rows * GROUP, HD), F32),
            pltpu.VMEM((rows, GROUP, HD), BF16),
            pltpu.VMEM((rows, GROUP, HD), BF16),
            pltpu.VMEM((rows, 4, HD), F32),
            pltpu.VMEM((rows, 4, HD), F32),
            pltpu.VMEM((rows, GROUP, HD), BF16),
            pltpu.VMEM((ROWS_STEP * GROUP, ROWS_STEP * HD), BF16),
            pltpu.VMEM((rows, GROUP, HD), BF16),
            pltpu.VMEM((rows, GROUP, HD), BF16),
            pltpu.VMEM((rows, GROUP, HD), BF16),
            pltpu.VMEM((n_kvh, share, out_cols), F32),
            pltpu.VMEM((n_kvh, share, out_cols), F32),
            dma((10,)),
            dma((7,)),
            dma((7,)),
            dma((rows // ROWS_STEP,)),
        ],
        compiler_params=pltpu.CompilerParams(
            collective_id=0, has_side_effects=True, vmem_limit_bytes=40 * 1024 * 1024
        ),
        name="decode_step",
    )(
        *(
            pltpu.with_memory_space_constraint(a, pltpu.HBM)
            for a in (
                lengths, positions, jnp.asarray(rotary_table()), inputs,
                w_query, w_key, w_value, w_output, keys, values,
            )
        )
    )


def solution(mesh):
    return jax.shard_map(
        body,
        mesh=mesh,
        in_specs=(
            P("kvh", "seq"),
            P("seq", "kvh"),
            P("seq", "kvh"),
            P("seq", "kvh"),
            P("kvh", "seq"),
            P(None, "seq", "kvh", None),
            P(None, "seq", "kvh", None),
            P(None),
            P(None),
        ),
        out_specs=P("kvh", "seq"),
        check_vma=False,
    )
```

```python
import jax
import jax.numpy as jnp
import numpy as np
from jax import lax
from jax.experimental import pallas as pl
from jax.experimental.pallas import tpu as pltpu
from jax.sharding import PartitionSpec as P

QH = 128
KVH = 8
HD = 128
GROUP = QH // KVH
MESH = pl.DeviceIdType.MESH
F32 = jnp.float32
BF16 = jnp.bfloat16
ROWS_STEP = 8


def rotary_table():
    half = HD // 2
    freq = 500000.0 ** (-np.arange(half, dtype=np.float64) * 2.0 / HD)
    return np.tile(freq.astype(np.float32), 2).reshape(1, HD)


def hops(offset, sizes):
    return sum(min(d, n - d) for d, n in zip(offset, sizes))


def by_distance(sizes):
    return sorted(np.ndindex(*sizes), key=lambda o: hops(o, sizes))


SEQ_SIZES = (4, 8)
KVH_SIZES = (4, 2)
SEQ_OFFSETS = by_distance(SEQ_SIZES)
KVH_OFFSETS = by_distance(KVH_SIZES)


def peer(index, offset, sizes):
    outer, inner = sizes
    return ((index // inner + offset[0]) % outer) * inner + (index % inner + offset[1]) % inner


def kernel(
    lengths_hbm, positions_hbm, freq_hbm, inputs, wq_hbm, wk_hbm, wv_hbm, wo_hbm, key_hbm, value_hbm,
    out_ref,
    lengths, positions, freq, x_own, wq, wk, wv, wo, keys, values,
    x_all, rel, q_send, q_recv, stat_send, stat_recv, q_all, q_block,
    part_send, part_recv, heads_all, out_send, out_recv,
    load_sem, send_sem, recv_sem, group_sem, entry_sem,
):
    seq = lax.axis_index("seq")
    kvh = lax.axis_index("kvh")
    n_seq = len(SEQ_OFFSETS)
    n_kvh = len(KVH_OFFSETS)
    rows = q_all.shape[0]
    share = x_own.shape[0]
    block = keys.shape[1]
    scale = HD ** (-0.5)
    lanes = ROWS_STEP * GROUP
    seq_peers = [peer(seq, o, SEQ_SIZES) for o in SEQ_OFFSETS]
    kvh_peers = [peer(kvh, o, KVH_SIZES) for o in KVH_OFFSETS]
    place_of = {o: p for p, o in enumerate(SEQ_OFFSETS)}
    back = [place_of[tuple(-d % n for d, n in zip(o, SEQ_SIZES))] for o in SEQ_OFFSETS]
    near = [p for p in range(n_seq - 1, 0, -1) if hops(SEQ_OFFSETS[p], SEQ_SIZES) <= 3]
    far_first = list(range(n_seq - 1, 0, -1))

    def load(src, dst, n):
        copy = pltpu.make_async_copy(src, dst, load_sem.at[n])
        copy.start()
        return copy

    x_load = load(inputs, x_own, 0)
    small = [load(positions_hbm, positions, 1), load(freq_hbm, freq, 2), load(lengths_hbm, lengths, 3)]
    wk_load = load(wk_hbm, wk, 4)
    wv_load = load(wv_hbm, wv, 5)
    wq_load = load(wq_hbm, wq, 6)
    key_load = load(key_hbm, keys, 7)
    value_load = load(value_hbm, values, 8)
    wo_load = load(wo_hbm, wo, 9)

    barrier = pltpu.get_barrier_semaphore()
    for p in near:
        pl.semaphore_signal(barrier, inc=1, device_id={"seq": seq_peers[p]}, device_id_type=MESH)
    for p in range(n_kvh - 1, 0, -1):
        pl.semaphore_signal(barrier, inc=1, device_id={"kvh": kvh_peers[p]}, device_id_type=MESH)
    q_block[...] = jnp.zeros_like(q_block)
    pl.semaphore_wait(barrier, len(near) + n_kvh - 1)

    def tell(step):
        for p in near:
            pl.semaphore_signal(entry_sem.at[step], inc=1, device_id={"seq": seq_peers[p]}, device_id_type=MESH)

    tell(0)
    x_load.wait()
    x_all[kvh] = x_own[...].astype(F32)

    def send(axis, to, src, dst, phase, arrived):
        pltpu.make_async_remote_copy(
            src_ref=src, dst_ref=dst, send_sem=send_sem.at[phase], recv_sem=arrived,
            device_id={axis: to}, device_id_type=MESH,
        ).start()

    def sums_of(ref, count, phase, arrived):
        return pltpu.make_async_remote_copy(
            src_ref=ref.at[pl.ds(0, count)], dst_ref=ref.at[pl.ds(0, count)],
            send_sem=send_sem.at[phase], recv_sem=arrived,
            device_id={"kvh": kvh_peers[1]}, device_id_type=MESH,
        )

    def received(ref, count, phase):
        sums_of(ref, count, phase, recv_sem.at[phase]).wait_recv()

    def sent(ref, count, phase):
        sums_of(ref, count, phase, recv_sem.at[phase]).wait_send()

    for p in range(n_kvh - 1, 0, -1):
        send("kvh", kvh_peers[p], x_all.at[kvh], x_all.at[kvh], 0, recv_sem.at[0])

    for copy in small:
        copy.wait()
    angle = positions[seq].astype(F32) * freq[...]
    cosine = jnp.cos(angle)
    sine = jnp.sin(angle)
    lane = lax.broadcasted_iota(jnp.int32, (1, HD), 1)
    sine = jnp.where(lane < HD // 2, -sine, sine)

    def rotate(t):
        return t * cosine + pltpu.roll(t, HD // 2, 1) * sine

    wk_load.wait()
    wv_load.wait()
    wq_load.wait()
    received(x_all, n_kvh - 1, 0)
    x = jnp.concatenate([x_all[i] for i in range(n_kvh)], axis=0).astype(BF16)

    for c in range(0, GROUP, 2):
        part = jnp.dot(x, wq[:, c * HD : (c + 2) * HD], preferred_element_type=F32)
        rel[pl.ds(c, rows, stride=GROUP), :] = part[:, :HD]
        rel[pl.ds(c + 1, rows, stride=GROUP), :] = part[:, HD:]
    q_send[...] = rel[...].astype(BF16).reshape(q_send.shape)

    pl.semaphore_wait(entry_sem.at[0], len(near))
    for p in far_first:
        to = seq_peers[p]
        send("seq", to, q_send.at[to], q_recv.at[seq], 1, recv_sem.at[1])
    q_recv[seq] = q_send[seq]
    k_part = jnp.dot(x, wk[...], preferred_element_type=F32)
    v_part = jnp.dot(x, wv[...], preferred_element_type=F32)
    for r in range(rows):
        stat_send[r, 2:3, :] = k_part[r : r + 1, :]
        stat_send[r, 3:4, :] = v_part[r : r + 1, :]
    received(q_recv, n_seq - 1, 1)
    q_own = rotate(jnp.sum(q_recv[...].astype(F32), axis=0)).astype(BF16)
    q_all[seq] = q_own

    for p in far_first:
        send("seq", seq_peers[p], q_all.at[seq], q_all.at[seq], 2, group_sem.at[back[p] // ROWS_STEP])
    sent(x_all, n_kvh - 1, 0)
    sent(q_send, n_seq - 1, 1)

    place = seq * block + lax.broadcasted_iota(jnp.int32, (GROUP, block), 1)
    lane_of = lax.broadcasted_iota(jnp.int32, (lanes, lanes), 1)
    key_load.wait()
    value_load.wait()
    for g in range(rows // ROWS_STEP):
        here = seq_peers[g * ROWS_STEP : (g + 1) * ROWS_STEP]
        sums_of(q_all, ROWS_STEP - (g == 0), 2, group_sem.at[g]).wait_recv()
        pieces = []
        for j in range(0, ROWS_STEP, 2):
            q_block[j * GROUP : (j + 1) * GROUP, :HD] = q_all[here[j]]
            q_block[(j + 1) * GROUP : (j + 2) * GROUP, HD:] = q_all[here[j + 1]]
            k_cat = jnp.concatenate([keys[here[j]], keys[here[j + 1]]], axis=1)
            pieces.append(lax.dot_general(
                q_block[j * GROUP : (j + 2) * GROUP], k_cat, (((1,), (1,)), ((), ())), preferred_element_type=F32
            ))
        scores = jnp.concatenate(pieces, axis=0) * scale
        valid = jnp.concatenate([place < lengths[row] for row in here], axis=0)
        masked = jnp.where(valid, scores, F32(-1e30))
        block_max = jnp.max(masked, axis=1, keepdims=True)
        weights = jnp.where(valid, jnp.exp(masked - block_max), F32(0.0))
        total = jnp.sum(weights, axis=1, keepdims=True)
        turned = weights.astype(BF16)
        for j in range(0, ROWS_STEP, 2):
            v_cat = jnp.concatenate([values[here[j]], values[here[j + 1]]], axis=1)
            got = jnp.dot(
                turned[j * GROUP : (j + 2) * GROUP], v_cat, preferred_element_type=F32
            ).astype(BF16)
            part_send[here[j]] = got[:GROUP, :HD]
            part_send[here[j + 1]] = got[GROUP:, HD:]
        stats = jnp.where(lane_of == 0, block_max, total).T[:2]
        for j, row in enumerate(here):
            stat_send[row, 0:2, :] = pltpu.roll(stats, (lanes - j * GROUP) % lanes, 1)
        for p in range((g + 1) * ROWS_STEP - 1, max(g * ROWS_STEP, 1) - 1, -1):
            to = seq_peers[p]
            send("seq", to, part_send.at[to], part_recv.at[seq], 3, recv_sem.at[3])
            send("seq", to, stat_send.at[to], stat_recv.at[seq], 4, recv_sem.at[4])

    part_recv[seq] = part_send[seq]
    stat_recv[seq] = stat_send[seq]
    sent(q_all, n_seq - 1, 2)
    received(stat_recv, n_seq - 1, 4)
    stats = stat_recv[...]
    k_new = rotate(jnp.sum(stats[:, 2, :], axis=0, keepdims=True)).astype(BF16).astype(F32)
    v_new = jnp.sum(stats[:, 3, :], axis=0, keepdims=True).astype(BF16).astype(F32)
    new_score = jnp.sum(q_own.astype(F32) * k_new, axis=1, keepdims=True) * scale
    maxima = stats[:, 0, :].T[:GROUP]
    totals = stats[:, 1, :].T[:GROUP]
    top = jnp.maximum(jnp.max(maxima, axis=1, keepdims=True), new_score)
    factor = jnp.exp(maxima - top)
    own = jnp.exp(new_score - top)
    total = jnp.sum(factor * totals, axis=1, keepdims=True) + own
    summed = own * v_new
    received(part_recv, n_seq - 1, 3)
    for s in range(rows):
        summed = summed + factor[:, s : s + 1] * part_recv[s].astype(F32)
    heads_all[seq] = (summed / total).astype(BF16)

    for p in far_first:
        send("seq", seq_peers[p], heads_all.at[seq], heads_all.at[seq], 5, recv_sem.at[5])
    sent(part_send, n_seq - 1, 3)
    sent(stat_send, n_seq - 1, 4)
    wo_load.wait()
    received(heads_all, n_seq - 1, 5)
    rel[...] = heads_all[...].reshape(rel.shape).astype(F32)
    heads = jnp.concatenate(
        [rel[pl.ds(h, rows, stride=GROUP), :].astype(BF16) for h in range(GROUP)], axis=1
    )
    terms = jnp.dot(heads, wo[...], preferred_element_type=F32)
    for i in range(rows // share):
        out_send[i] = terms[i * share : (i + 1) * share, :]

    for p in range(n_kvh - 1, 0, -1):
        to = kvh_peers[p]
        send("kvh", to, out_send.at[to], out_recv.at[kvh], 6, recv_sem.at[6])
    out_recv[kvh] = out_send[kvh]
    sent(heads_all, n_seq - 1, 5)
    received(out_recv, n_kvh - 1, 6)
    out_ref[...] = jnp.sum(out_recv[...], axis=0).astype(out_ref.dtype)
    sent(out_send, n_kvh - 1, 6)


def body(inputs, w_query, w_key, w_value, w_output, key_cache, value_cache, lengths, positions):
    n_kvh = lax.axis_size("kvh")
    share, depth = inputs.shape
    rows, block = key_cache.shape[:2]
    out_cols = w_output.shape[1]
    keys = jnp.transpose(key_cache, (0, 2, 1, 3)).reshape(rows, block, HD)
    values = jnp.transpose(value_cache, (0, 2, 1, 3)).reshape(rows, block, HD)
    vmem = pl.BlockSpec(memory_space=pltpu.VMEM)
    hbm = pl.BlockSpec(memory_space=pltpu.HBM)
    dma = pltpu.SemaphoreType.DMA
    return pl.pallas_call(
        kernel,
        out_shape=jax.ShapeDtypeStruct((share, out_cols), BF16),
        in_specs=[hbm] * 10,
        out_specs=vmem,
        scratch_shapes=[
            pltpu.SMEM(lengths.shape, jnp.int32),
            pltpu.SMEM(positions.shape, jnp.int32),
            pltpu.VMEM((1, HD), F32),
            pltpu.VMEM((share, depth), BF16),
            pltpu.VMEM(w_query.shape, BF16),
            pltpu.VMEM(w_key.shape, BF16),
            pltpu.VMEM(w_value.shape, BF16),
            pltpu.VMEM(w_output.shape, BF16),
            pltpu.VMEM(keys.shape, BF16),
            pltpu.VMEM(values.shape, BF16),
            pltpu.VMEM((n_kvh, share, depth), F32),
            pltpu.VMEM((rows * GROUP, HD), F32),
            pltpu.VMEM((rows, GROUP, HD), BF16),
            pltpu.VMEM((rows, GROUP, HD), BF16),
            pltpu.VMEM((rows, 4, HD), F32),
            pltpu.VMEM((rows, 4, HD), F32),
            pltpu.VMEM((rows, GROUP, HD), BF16),
            pltpu.VMEM((ROWS_STEP * GROUP, 2 * HD), BF16),
            pltpu.VMEM((rows, GROUP, HD), BF16),
            pltpu.VMEM((rows, GROUP, HD), BF16),
            pltpu.VMEM((rows, GROUP, HD), BF16),
            pltpu.VMEM((n_kvh, share, out_cols), F32),
            pltpu.VMEM((n_kvh, share, out_cols), F32),
            dma((10,)),
            dma((7,)),
            dma((7,)),
            dma((rows // ROWS_STEP,)),
            pltpu.SemaphoreType.REGULAR((1,)),
        ],
        compiler_params=pltpu.CompilerParams(
            collective_id=0, has_side_effects=True, vmem_limit_bytes=40 * 1024 * 1024
        ),
        name="decode_step",
    )(
        *(
            pltpu.with_memory_space_constraint(a, pltpu.HBM)
            for a in (
                lengths, positions, jnp.asarray(rotary_table()), inputs,
                w_query, w_key, w_value, w_output, keys, values,
            )
        )
    )


def solution(mesh):
    return jax.shard_map(
        body,
        mesh=mesh,
        in_specs=(
            P("kvh", "seq"),
            P("seq", "kvh"),
            P("seq", "kvh"),
            P("seq", "kvh"),
            P("kvh", "seq"),
            P(None, "seq", "kvh", None),
            P(None, "seq", "kvh", None),
            P(None),
            P(None),
        ),
        out_specs=P("kvh", "seq"),
        check_vma=False,
    )
```

```python
import jax
import jax.numpy as jnp
import numpy as np
from jax import lax
from jax.experimental import pallas as pl
from jax.experimental.pallas import tpu as pltpu
from jax.sharding import PartitionSpec as P

QH = 128
KVH = 8
HD = 128
GROUP = QH // KVH
MESH = pl.DeviceIdType.MESH
F32 = jnp.float32
BF16 = jnp.bfloat16
ROWS_STEP = 8
HALF = 16


def rotary_table():
    half = HD // 2
    freq = 500000.0 ** (-np.arange(half, dtype=np.float64) * 2.0 / HD)
    return np.tile(freq.astype(np.float32), 2).reshape(1, HD)


def hops(offset, sizes):
    return sum(min(d, n - d) for d, n in zip(offset, sizes))


def by_distance(sizes):
    return sorted(np.ndindex(*sizes), key=lambda o: hops(o, sizes))


SEQ_SIZES = (4, 8)
KVH_SIZES = (4, 2)
SEQ_OFFSETS = by_distance(SEQ_SIZES)
KVH_OFFSETS = by_distance(KVH_SIZES)


def peer(index, offset, sizes):
    outer, inner = sizes
    return ((index // inner + offset[0]) % outer) * inner + (index % inner + offset[1]) % inner


def kernel(
    lengths_hbm, positions_hbm, freq_hbm, inputs, wq_hbm, wk_hbm, wv_hbm, wo_hbm, key_hbm, value_hbm,
    out_ref,
    lengths, positions, freq, x_own, wq, wk, wv, wo, keys, values,
    x_all, rel, q_send, q_recv, stat_send, stat_recv, q_all, q_block,
    part_send, part_recv, heads_all, out_send, out_recv,
    load_sem, send_sem, recv_sem, group_sem, part_sem, stat_sem, heads_sem, entry_sem,
):
    seq = lax.axis_index("seq")
    kvh = lax.axis_index("kvh")
    n_seq = len(SEQ_OFFSETS)
    n_kvh = len(KVH_OFFSETS)
    rows = q_all.shape[0]
    share = x_own.shape[0]
    block = keys.shape[1]
    scale = HD ** (-0.5)
    lanes = ROWS_STEP * GROUP
    seq_peers = [peer(seq, o, SEQ_SIZES) for o in SEQ_OFFSETS]
    kvh_peers = [peer(kvh, o, KVH_SIZES) for o in KVH_OFFSETS]
    place_of = {o: p for p, o in enumerate(SEQ_OFFSETS)}
    back = [place_of[tuple(-d % n for d, n in zip(o, SEQ_SIZES))] for o in SEQ_OFFSETS]
    near = [p for p in range(n_seq - 1, 0, -1) if hops(SEQ_OFFSETS[p], SEQ_SIZES) <= 3]
    far_first = list(range(n_seq - 1, 0, -1))
    distance = [hops(o, SEQ_SIZES) for o in SEQ_OFFSETS]
    gather_order = sorted(far_first, key=lambda p: (distance[p] < 5, distance[p] > 2, distance[p]))

    def load(src, dst, n):
        copy = pltpu.make_async_copy(src, dst, load_sem.at[n])
        copy.start()
        return copy

    x_load = load(inputs, x_own, 0)
    small = [load(positions_hbm, positions, 1), load(freq_hbm, freq, 2), load(lengths_hbm, lengths, 3)]
    wk_load = load(wk_hbm, wk, 4)
    wv_load = load(wv_hbm, wv, 5)
    wq_load = load(wq_hbm, wq, 6)
    key_load = load(key_hbm, keys, 7)
    value_load = load(value_hbm, values, 8)
    wo_load = load(wo_hbm, wo, 9)

    barrier = pltpu.get_barrier_semaphore()
    for p in range(n_kvh - 1, 0, -1):
        pl.semaphore_signal(barrier, inc=1, device_id={"kvh": kvh_peers[p]}, device_id_type=MESH)
    for p in near:
        pl.semaphore_signal(barrier, inc=1, device_id={"seq": seq_peers[p]}, device_id_type=MESH)
    q_block[...] = jnp.zeros_like(q_block)
    x_load.wait()
    x_all[kvh] = x_own[...].astype(F32)
    pl.semaphore_wait(barrier, len(near) + n_kvh - 1)

    def tell(step):
        for p in near:
            pl.semaphore_signal(entry_sem.at[step], inc=1, device_id={"seq": seq_peers[p]}, device_id_type=MESH)

    def send(axis, to, src, dst, phase, arrived):
        pltpu.make_async_remote_copy(
            src_ref=src, dst_ref=dst, send_sem=send_sem.at[phase], recv_sem=arrived,
            device_id={axis: to}, device_id_type=MESH,
        ).start()

    def sums_of(ref, count, phase, arrived):
        return pltpu.make_async_remote_copy(
            src_ref=ref.at[pl.ds(0, count)], dst_ref=ref.at[pl.ds(0, count)],
            send_sem=send_sem.at[phase], recv_sem=arrived,
            device_id={"kvh": kvh_peers[1]}, device_id_type=MESH,
        )

    def received(ref, count, phase):
        sums_of(ref, count, phase, recv_sem.at[phase]).wait_recv()

    def sent(ref, count, phase):
        sums_of(ref, count, phase, recv_sem.at[phase]).wait_send()

    for p in range(n_kvh - 1, 0, -1):
        send("kvh", kvh_peers[p], x_all.at[kvh], x_all.at[kvh], 0, recv_sem.at[0])
    tell(0)

    for copy in small:
        copy.wait()
    angle = positions[seq].astype(F32) * freq[...]
    cosine = jnp.cos(angle)
    sine = jnp.sin(angle)
    lane = lax.broadcasted_iota(jnp.int32, (1, HD), 1)
    sine = jnp.where(lane < HD // 2, -sine, sine)

    def rotate(t):
        return t * cosine + pltpu.roll(t, HD // 2, 1) * sine

    wk_load.wait()
    wv_load.wait()
    wq_load.wait()
    received(x_all, n_kvh - 1, 0)
    x = jnp.concatenate([x_all[i] for i in range(n_kvh)], axis=0).astype(BF16)

    for c in range(0, GROUP, 2):
        part = jnp.dot(x, wq[:, c * HD : (c + 2) * HD], preferred_element_type=F32)
        rel[pl.ds(c, rows, stride=GROUP), :] = part[:, :HD]
        rel[pl.ds(c + 1, rows, stride=GROUP), :] = part[:, HD:]
    q_send[...] = rel[...].astype(BF16).reshape(q_send.shape)

    pl.semaphore_wait(entry_sem.at[0], len(near))
    for p in far_first:
        to = seq_peers[p]
        send("seq", to, q_send.at[to], q_recv.at[seq], 1, recv_sem.at[1])
    q_recv[seq] = q_send[seq]
    k_part = jnp.dot(x, wk[...], preferred_element_type=F32)
    v_part = jnp.dot(x, wv[...], preferred_element_type=F32)
    for r in range(rows):
        stat_send[r, 2:3, :] = k_part[r : r + 1, :]
        stat_send[r, 3:4, :] = v_part[r : r + 1, :]
    received(q_recv, n_seq - 1, 1)
    q_own = rotate(jnp.sum(q_recv[...].astype(F32), axis=0)).astype(BF16)
    q_all[seq] = q_own

    for p in gather_order:
        send("seq", seq_peers[p], q_all.at[seq], q_all.at[seq], 2, group_sem.at[back[p] // ROWS_STEP])
    sent(x_all, n_kvh - 1, 0)
    sent(q_send, n_seq - 1, 1)

    place = seq * block + lax.broadcasted_iota(jnp.int32, (GROUP, block), 1)
    lane_of = lax.broadcasted_iota(jnp.int32, (lanes, lanes), 1)
    key_load.wait()
    value_load.wait()
    groups = rows // ROWS_STEP
    for g in range(groups):
        here = seq_peers[g * ROWS_STEP : (g + 1) * ROWS_STEP]
        sums_of(q_all, ROWS_STEP - (g == 0), 2, group_sem.at[g]).wait_recv()
        pieces = []
        for j in range(0, ROWS_STEP, 2):
            q_block[j * GROUP : (j + 1) * GROUP, :HD] = q_all[here[j]]
            q_block[(j + 1) * GROUP : (j + 2) * GROUP, HD:] = q_all[here[j + 1]]
            k_cat = jnp.concatenate([keys[here[j]], keys[here[j + 1]]], axis=1)
            pieces.append(lax.dot_general(
                q_block[j * GROUP : (j + 2) * GROUP], k_cat, (((1,), (1,)), ((), ())), preferred_element_type=F32
            ))
        scores = jnp.concatenate(pieces, axis=0) * scale
        valid = jnp.concatenate([place < lengths[row] for row in here], axis=0)
        masked = jnp.where(valid, scores, F32(-1e30))
        block_max = jnp.max(masked, axis=1, keepdims=True)
        weights = jnp.where(valid, jnp.exp(masked - block_max), F32(0.0))
        total = jnp.sum(weights, axis=1, keepdims=True)
        turned = weights.astype(BF16)
        for j in range(0, ROWS_STEP, 2):
            v_cat = jnp.concatenate([values[here[j]], values[here[j + 1]]], axis=1)
            got = jnp.dot(
                turned[j * GROUP : (j + 2) * GROUP], v_cat, preferred_element_type=F32
            ).astype(BF16)
            part_send[here[j]] = got[:GROUP, :HD]
            part_send[here[j + 1]] = got[GROUP:, HD:]
        stats = jnp.where(lane_of == 0, block_max, total).T[:2]
        for j, row in enumerate(here):
            stat_send[row, 0:2, :] = pltpu.roll(stats, (lanes - j * GROUP) % lanes, 1)
        last = g == groups - 1
        for p in range((g + 1) * ROWS_STEP - 1, max(g * ROWS_STEP, 1) - 1, -1):
            to = seq_peers[p]
            send("seq", to, part_send.at[to], part_recv.at[back[p]], 3, part_sem.at[back[p] // HALF])
            if last:
                send("seq", to, stat_send.at[to], stat_recv.at[back[p]], 4, stat_sem.at[back[p] // HALF])
    for p in far_first[ROWS_STEP:]:
        to = seq_peers[p]
        send("seq", to, stat_send.at[to], stat_recv.at[back[p]], 4, stat_sem.at[back[p] // HALF])

    part_recv[0] = part_send[seq]
    stat_recv[0] = stat_send[seq]
    sent(q_all, n_seq - 1, 2)
    top = total = summed = None
    for wave in range(2):
        first = wave * HALF
        count = HALF - (wave == 0)
        sums_of(stat_recv, count, 4, stat_sem.at[wave]).wait_recv()
        stats = stat_recv[first : first + HALF]
        maxima = stats[:, 0, :].T[:GROUP]
        totals = stats[:, 1, :].T[:GROUP]
        k_new = jnp.sum(stats[:, 2, :], axis=0, keepdims=True) + (k_new if wave else 0.0)
        v_new = jnp.sum(stats[:, 3, :], axis=0, keepdims=True) + (v_new if wave else 0.0)
        here_top = jnp.max(maxima, axis=1, keepdims=True)
        if wave:
            k_new = rotate(k_new).astype(BF16).astype(F32)
            v_new = v_new.astype(BF16).astype(F32)
            new_score = jnp.sum(q_own.astype(F32) * k_new, axis=1, keepdims=True) * scale
            here_top = jnp.maximum(jnp.maximum(here_top, new_score), top)
            kept = jnp.exp(top - here_top)
            own = jnp.exp(new_score - here_top)
            total = total * kept + own
            summed = summed * kept + own * v_new
        top = here_top
        factor = jnp.exp(maxima - top)
        here_total = jnp.sum(factor * totals, axis=1, keepdims=True)
        total = total + here_total if wave else here_total
        sums_of(part_recv, count, 3, part_sem.at[wave]).wait_recv()
        for s in range(HALF):
            term = factor[:, s : s + 1] * part_recv[first + s].astype(F32)
            summed = term if summed is None else summed + term
    heads_all[seq] = (summed / total).astype(BF16)

    outer, inner = SEQ_SIZES
    y = seq // inner
    half = seq % inner // share

    def urgency(p):
        dy = min(SEQ_OFFSETS[p][0], outer - SEQ_OFFSETS[p][0])
        return (distance[p] != 4 or dy == 2, distance[p] < 5, distance[p] != 3, -distance[p])

    for p in sorted(far_first, key=urgency):
        dy = SEQ_OFFSETS[p][0]
        to = seq_peers[p]
        if dy == 0:
            wave = 0
        elif dy in (1, outer - 1):
            wave = (half + to % inner // share) % 2
        else:
            wave = 1
        send("seq", to, heads_all.at[seq], heads_all.at[seq], 5, heads_sem.at[wave])
    sent(part_send, n_seq - 1, 3)
    sent(stat_send, n_seq - 1, 4)
    wo_load.wait()
    blocks = [
        [(0, 0), (0, 1), (1, 0), (outer - 1, 0)],
        [(1, 1), (outer - 1, 1), (2, 0), (2, 1)],
    ]
    for wave in range(2):
        quads = [(y + dy) % outer * 2 + (half + dh) % 2 for dy, dh in blocks[wave]]
        sums_of(heads_all, HALF - (wave == 0), 5, heads_sem.at[wave]).wait_recv()
        for i, quad in enumerate(quads):
            rel[i * share * GROUP : (i + 1) * share * GROUP] = (
                heads_all[pl.ds(quad * share, share)].reshape(share * GROUP, HD).astype(F32)
            )
        heads = jnp.concatenate(
            [rel[pl.ds(h, HALF, stride=GROUP), :].astype(BF16) for h in range(GROUP)], axis=1
        )
        terms = jnp.dot(heads, wo[...], preferred_element_type=F32)
        for i, quad in enumerate(quads):
            out_send[quad] = terms[i * share : (i + 1) * share, :]
        for quad in quads:

            @pl.when(quad != kvh)
            def _():
                send("kvh", quad, out_send.at[quad], out_recv.at[kvh], 6, recv_sem.at[6])

    out_recv[kvh] = out_send[kvh]
    sent(heads_all, n_seq - 1, 5)
    received(out_recv, n_kvh - 1, 6)
    out_ref[...] = jnp.sum(out_recv[...], axis=0).astype(out_ref.dtype)
    sent(out_send, n_kvh - 1, 6)


def body(inputs, w_query, w_key, w_value, w_output, key_cache, value_cache, lengths, positions):
    n_kvh = lax.axis_size("kvh")
    share, depth = inputs.shape
    rows, block = key_cache.shape[:2]
    out_cols = w_output.shape[1]
    keys = jnp.transpose(key_cache, (0, 2, 1, 3)).reshape(rows, block, HD)
    values = jnp.transpose(value_cache, (0, 2, 1, 3)).reshape(rows, block, HD)
    vmem = pl.BlockSpec(memory_space=pltpu.VMEM)
    hbm = pl.BlockSpec(memory_space=pltpu.HBM)
    dma = pltpu.SemaphoreType.DMA
    return pl.pallas_call(
        kernel,
        out_shape=jax.ShapeDtypeStruct((share, out_cols), BF16),
        in_specs=[hbm] * 10,
        out_specs=vmem,
        scratch_shapes=[
            pltpu.SMEM(lengths.shape, jnp.int32),
            pltpu.SMEM(positions.shape, jnp.int32),
            pltpu.VMEM((1, HD), F32),
            pltpu.VMEM((share, depth), BF16),
            pltpu.VMEM(w_query.shape, BF16),
            pltpu.VMEM(w_key.shape, BF16),
            pltpu.VMEM(w_value.shape, BF16),
            pltpu.VMEM(w_output.shape, BF16),
            pltpu.VMEM(keys.shape, BF16),
            pltpu.VMEM(values.shape, BF16),
            pltpu.VMEM((n_kvh, share, depth), F32),
            pltpu.VMEM((rows * GROUP, HD), F32),
            pltpu.VMEM((rows, GROUP, HD), BF16),
            pltpu.VMEM((rows, GROUP, HD), BF16),
            pltpu.VMEM((rows, 4, HD), F32),
            pltpu.VMEM((rows, 4, HD), F32),
            pltpu.VMEM((rows, GROUP, HD), BF16),
            pltpu.VMEM((ROWS_STEP * GROUP, 2 * HD), BF16),
            pltpu.VMEM((rows, GROUP, HD), BF16),
            pltpu.VMEM((rows, GROUP, HD), BF16),
            pltpu.VMEM((rows, GROUP, HD), BF16),
            pltpu.VMEM((n_kvh, share, out_cols), F32),
            pltpu.VMEM((n_kvh, share, out_cols), F32),
            dma((10,)),
            dma((7,)),
            dma((7,)),
            dma((rows // ROWS_STEP,)),
            dma((2,)),
            dma((2,)),
            dma((2,)),
            pltpu.SemaphoreType.REGULAR((1,)),
        ],
        compiler_params=pltpu.CompilerParams(
            collective_id=0, has_side_effects=True, vmem_limit_bytes=40 * 1024 * 1024
        ),
        name="decode_step",
    )(
        *(
            pltpu.with_memory_space_constraint(a, pltpu.HBM)
            for a in (
                lengths, positions, jnp.asarray(rotary_table()), inputs,
                w_query, w_key, w_value, w_output, keys, values,
            )
        )
    )


def solution(mesh):
    return jax.shard_map(
        body,
        mesh=mesh,
        in_specs=(
            P("kvh", "seq"),
            P("seq", "kvh"),
            P("seq", "kvh"),
            P("seq", "kvh"),
            P("kvh", "seq"),
            P(None, "seq", "kvh", None),
            P(None, "seq", "kvh", None),
            P(None),
            P(None),
        ),
        out_specs=P("kvh", "seq"),
        check_vma=False,
    )
```

```python
import jax
import jax.numpy as jnp
import numpy as np
from jax import lax
from jax.experimental import pallas as pl
from jax.experimental.pallas import tpu as pltpu
from jax.sharding import PartitionSpec as P

QH = 128
KVH = 8
HD = 128
GROUP = QH // KVH
MESH = pl.DeviceIdType.MESH
F32 = jnp.float32
BF16 = jnp.bfloat16
ROWS_STEP = 8
HALF = 16


def rotary_table():
    half = HD // 2
    freq = 500000.0 ** (-np.arange(half, dtype=np.float64) * 2.0 / HD)
    return np.tile(freq.astype(np.float32), 2).reshape(1, HD)


def hops(offset, sizes):
    return sum(min(d, n - d) for d, n in zip(offset, sizes))


def by_distance(sizes):
    return sorted(np.ndindex(*sizes), key=lambda o: hops(o, sizes))


SEQ_SIZES = (4, 8)
KVH_SIZES = (4, 2)
SEQ_OFFSETS = by_distance(SEQ_SIZES)
KVH_OFFSETS = by_distance(KVH_SIZES)


def peer(index, offset, sizes):
    outer, inner = sizes
    return ((index // inner + offset[0]) % outer) * inner + (index % inner + offset[1]) % inner


def kernel(
    lengths_hbm, positions_hbm, freq_hbm, inputs, wq_hbm, wk_hbm, wv_hbm, wo_hbm, key_hbm, value_hbm,
    out_ref,
    lengths, positions, freq, x_own, wq, wk, wv, wo, keys, values,
    x_all, rel, q_send, q_recv, stat_send, stat_recv, q_all, q_block,
    part_send, part_recv, heads_all, out_send, out_recv,
    load_sem, send_sem, recv_sem, group_sem, part_sem, stat_sem, heads_sem, entry_sem,
):
    seq = lax.axis_index("seq")
    kvh = lax.axis_index("kvh")
    n_seq = len(SEQ_OFFSETS)
    n_kvh = len(KVH_OFFSETS)
    rows = q_all.shape[0]
    share = x_own.shape[0]
    block = keys.shape[1]
    scale = HD ** (-0.5)
    lanes = ROWS_STEP * GROUP
    seq_peers = [peer(seq, o, SEQ_SIZES) for o in SEQ_OFFSETS]
    kvh_peers = [peer(kvh, o, KVH_SIZES) for o in KVH_OFFSETS]
    place_of = {o: p for p, o in enumerate(SEQ_OFFSETS)}
    back = [place_of[tuple(-d % n for d, n in zip(o, SEQ_SIZES))] for o in SEQ_OFFSETS]
    near = [p for p in range(n_seq - 1, 0, -1) if hops(SEQ_OFFSETS[p], SEQ_SIZES) <= 3]
    far_first = list(range(n_seq - 1, 0, -1))
    distance = [hops(o, SEQ_SIZES) for o in SEQ_OFFSETS]
    turn = (0, 1, 3, 2)
    gather_order = sorted(far_first, key=lambda p: ((1, 2, 3, 0)[back[p] // ROWS_STEP], -distance[p]))

    def load(src, dst, n):
        copy = pltpu.make_async_copy(src, dst, load_sem.at[n])
        copy.start()
        return copy

    x_load = load(inputs, x_own, 0)
    small = [load(positions_hbm, positions, 1), load(freq_hbm, freq, 2), load(lengths_hbm, lengths, 3)]
    wk_load = load(wk_hbm, wk, 4)
    wv_load = load(wv_hbm, wv, 5)
    wq_load = load(wq_hbm, wq, 6)
    key_load = load(key_hbm, keys, 7)
    value_load = load(value_hbm, values, 8)
    wo_load = load(wo_hbm, wo, 9)

    barrier = pltpu.get_barrier_semaphore()
    for p in range(n_kvh - 1, 0, -1):
        pl.semaphore_signal(barrier, inc=1, device_id={"kvh": kvh_peers[p]}, device_id_type=MESH)
    for p in near:
        pl.semaphore_signal(barrier, inc=1, device_id={"seq": seq_peers[p]}, device_id_type=MESH)
    q_block[...] = jnp.zeros_like(q_block)
    x_load.wait()
    x_all[kvh] = x_own[...].astype(F32)
    pl.semaphore_wait(barrier, len(near) + n_kvh - 1)

    def tell(step):
        for p in near:
            pl.semaphore_signal(entry_sem.at[step], inc=1, device_id={"seq": seq_peers[p]}, device_id_type=MESH)

    def send(axis, to, src, dst, phase, arrived):
        pltpu.make_async_remote_copy(
            src_ref=src, dst_ref=dst, send_sem=send_sem.at[phase], recv_sem=arrived,
            device_id={axis: to}, device_id_type=MESH,
        ).start()

    def sums_of(ref, count, phase, arrived):
        return pltpu.make_async_remote_copy(
            src_ref=ref.at[pl.ds(0, count)], dst_ref=ref.at[pl.ds(0, count)],
            send_sem=send_sem.at[phase], recv_sem=arrived,
            device_id={"kvh": kvh_peers[1]}, device_id_type=MESH,
        )

    def received(ref, count, phase):
        sums_of(ref, count, phase, recv_sem.at[phase]).wait_recv()

    def sent(ref, count, phase):
        sums_of(ref, count, phase, recv_sem.at[phase]).wait_send()

    for p in range(n_kvh - 1, 0, -1):
        send("kvh", kvh_peers[p], x_all.at[kvh], x_all.at[kvh], 0, recv_sem.at[0])
    tell(0)

    for copy in small:
        copy.wait()
    angle = positions[seq].astype(F32) * freq[...]
    cosine = jnp.cos(angle)
    sine = jnp.sin(angle)
    lane = lax.broadcasted_iota(jnp.int32, (1, HD), 1)
    sine = jnp.where(lane < HD // 2, -sine, sine)

    def rotate(t):
        return t * cosine + pltpu.roll(t, HD // 2, 1) * sine

    wk_load.wait()
    wv_load.wait()
    wq_load.wait()
    received(x_all, n_kvh - 1, 0)
    x = jnp.concatenate([x_all[i] for i in range(n_kvh)], axis=0).astype(BF16)

    for c in range(0, GROUP, 2):
        part = jnp.dot(x, wq[:, c * HD : (c + 2) * HD], preferred_element_type=F32)
        rel[pl.ds(c, rows, stride=GROUP), :] = part[:, :HD]
        rel[pl.ds(c + 1, rows, stride=GROUP), :] = part[:, HD:]
    q_send[...] = rel[...].astype(BF16).reshape(q_send.shape)

    pl.semaphore_wait(entry_sem.at[0], len(near))
    for p in far_first:
        to = seq_peers[p]
        send("seq", to, q_send.at[to], q_recv.at[seq], 1, recv_sem.at[1])
    q_recv[seq] = q_send[seq]
    k_part = jnp.dot(x, wk[...], preferred_element_type=F32)
    v_part = jnp.dot(x, wv[...], preferred_element_type=F32)
    for r in range(rows):
        stat_send[r, 2:3, :] = k_part[r : r + 1, :]
        stat_send[r, 3:4, :] = v_part[r : r + 1, :]
    received(q_recv, n_seq - 1, 1)
    q_own = rotate(jnp.sum(q_recv[...].astype(F32), axis=0)).astype(BF16)
    q_all[seq] = q_own

    for p in gather_order:
        send("seq", seq_peers[p], q_all.at[seq], q_all.at[seq], 2, group_sem.at[back[p] // ROWS_STEP])
    sent(x_all, n_kvh - 1, 0)
    sent(q_send, n_seq - 1, 1)

    place = seq * block + lax.broadcasted_iota(jnp.int32, (GROUP, block), 1)
    lane_of = lax.broadcasted_iota(jnp.int32, (lanes, lanes), 1)
    key_load.wait()
    value_load.wait()
    groups = rows // ROWS_STEP
    for g in turn:
        here = seq_peers[g * ROWS_STEP : (g + 1) * ROWS_STEP]
        sums_of(q_all, ROWS_STEP - (g == 0), 2, group_sem.at[g]).wait_recv()
        pieces = []
        for j in range(0, ROWS_STEP, 2):
            q_block[j * GROUP : (j + 1) * GROUP, :HD] = q_all[here[j]]
            q_block[(j + 1) * GROUP : (j + 2) * GROUP, HD:] = q_all[here[j + 1]]
            k_cat = jnp.concatenate([keys[here[j]], keys[here[j + 1]]], axis=1)
            pieces.append(lax.dot_general(
                q_block[j * GROUP : (j + 2) * GROUP], k_cat, (((1,), (1,)), ((), ())), preferred_element_type=F32
            ))
        scores = jnp.concatenate(pieces, axis=0) * scale
        valid = jnp.concatenate([place < lengths[row] for row in here], axis=0)
        masked = jnp.where(valid, scores, F32(-1e30))
        block_max = jnp.max(masked, axis=1, keepdims=True)
        weights = jnp.where(valid, jnp.exp(masked - block_max), F32(0.0))
        total = jnp.sum(weights, axis=1, keepdims=True)
        turned = weights.astype(BF16)
        for j in range(0, ROWS_STEP, 2):
            v_cat = jnp.concatenate([values[here[j]], values[here[j + 1]]], axis=1)
            got = jnp.dot(
                turned[j * GROUP : (j + 2) * GROUP], v_cat, preferred_element_type=F32
            ).astype(BF16)
            part_send[here[j]] = got[:GROUP, :HD]
            part_send[here[j + 1]] = got[GROUP:, HD:]
        stats = jnp.where(lane_of == 0, block_max, total).T[:2]
        for j, row in enumerate(here):
            stat_send[row, 0:2, :] = pltpu.roll(stats, (lanes - j * GROUP) % lanes, 1)
        late = g >= groups // 2
        for p in range((g + 1) * ROWS_STEP - 1, max(g * ROWS_STEP, 1) - 1, -1):
            to = seq_peers[p]
            send("seq", to, part_send.at[to], part_recv.at[back[p]], 3, part_sem.at[back[p] // HALF])
            if late:
                send("seq", to, stat_send.at[to], stat_recv.at[back[p]], 4, stat_sem.at[back[p] // HALF])
    for p in far_first[groups // 2 * ROWS_STEP :]:
        to = seq_peers[p]
        send("seq", to, stat_send.at[to], stat_recv.at[back[p]], 4, stat_sem.at[back[p] // HALF])

    part_recv[0] = part_send[seq]
    stat_recv[0] = stat_send[seq]
    sent(q_all, n_seq - 1, 2)
    top = total = summed = None
    for wave in range(2):
        first = wave * HALF
        count = HALF - (wave == 0)
        sums_of(stat_recv, count, 4, stat_sem.at[wave]).wait_recv()
        stats = stat_recv[first : first + HALF]
        maxima = stats[:, 0, :].T[:GROUP]
        totals = stats[:, 1, :].T[:GROUP]
        k_new = jnp.sum(stats[:, 2, :], axis=0, keepdims=True) + (k_new if wave else 0.0)
        v_new = jnp.sum(stats[:, 3, :], axis=0, keepdims=True) + (v_new if wave else 0.0)
        here_top = jnp.max(maxima, axis=1, keepdims=True)
        if wave:
            k_new = rotate(k_new).astype(BF16).astype(F32)
            v_new = v_new.astype(BF16).astype(F32)
            new_score = jnp.sum(q_own.astype(F32) * k_new, axis=1, keepdims=True) * scale
            here_top = jnp.maximum(jnp.maximum(here_top, new_score), top)
            kept = jnp.exp(top - here_top)
            own = jnp.exp(new_score - here_top)
            total = total * kept + own
            summed = summed * kept + own * v_new
        top = here_top
        factor = jnp.exp(maxima - top)
        here_total = jnp.sum(factor * totals, axis=1, keepdims=True)
        total = total + here_total if wave else here_total
        sums_of(part_recv, count, 3, part_sem.at[wave]).wait_recv()
        for s in range(HALF):
            term = factor[:, s : s + 1] * part_recv[first + s].astype(F32)
            summed = term if summed is None else summed + term
    heads_all[seq] = (summed / total).astype(BF16)

    outer, inner = SEQ_SIZES
    y = seq // inner
    half = seq % inner // share

    def urgency(p):
        dy = min(SEQ_OFFSETS[p][0], outer - SEQ_OFFSETS[p][0])
        return (distance[p] != 4 or dy == 2, distance[p] < 5, distance[p] != 3, -distance[p])

    for p in sorted(far_first, key=urgency):
        dy = SEQ_OFFSETS[p][0]
        to = seq_peers[p]
        if dy == 0:
            wave = 0
        elif dy in (1, outer - 1):
            wave = (half + to % inner // share) % 2
        else:
            wave = 1
        send("seq", to, heads_all.at[seq], heads_all.at[seq], 5, heads_sem.at[wave])
    sent(part_send, n_seq - 1, 3)
    sent(stat_send, n_seq - 1, 4)
    wo_load.wait()
    blocks = [
        [(0, 0), (0, 1), (1, 0), (outer - 1, 0)],
        [(1, 1), (outer - 1, 1), (2, 0), (2, 1)],
    ]
    for wave in range(2):
        quads = [(y + dy) % outer * 2 + (half + dh) % 2 for dy, dh in blocks[wave]]
        sums_of(heads_all, HALF - (wave == 0), 5, heads_sem.at[wave]).wait_recv()
        for i, quad in enumerate(quads):
            rel[i * share * GROUP : (i + 1) * share * GROUP] = (
                heads_all[pl.ds(quad * share, share)].reshape(share * GROUP, HD).astype(F32)
            )
        heads = jnp.concatenate(
            [rel[pl.ds(h, HALF, stride=GROUP), :].astype(BF16) for h in range(GROUP)], axis=1
        )
        terms = jnp.dot(heads, wo[...], preferred_element_type=F32)
        for i, quad in enumerate(quads):
            out_send[quad] = terms[i * share : (i + 1) * share, :]
        for quad in quads:

            @pl.when(quad != kvh)
            def _():
                send("kvh", quad, out_send.at[quad], out_recv.at[kvh], 6, recv_sem.at[6])

    out_recv[kvh] = out_send[kvh]
    sent(heads_all, n_seq - 1, 5)
    received(out_recv, n_kvh - 1, 6)
    out_ref[...] = jnp.sum(out_recv[...], axis=0).astype(out_ref.dtype)
    sent(out_send, n_kvh - 1, 6)


def body(inputs, w_query, w_key, w_value, w_output, key_cache, value_cache, lengths, positions):
    n_kvh = lax.axis_size("kvh")
    share, depth = inputs.shape
    rows, block = key_cache.shape[:2]
    out_cols = w_output.shape[1]
    keys = jnp.transpose(key_cache, (0, 2, 1, 3)).reshape(rows, block, HD)
    values = jnp.transpose(value_cache, (0, 2, 1, 3)).reshape(rows, block, HD)
    vmem = pl.BlockSpec(memory_space=pltpu.VMEM)
    hbm = pl.BlockSpec(memory_space=pltpu.HBM)
    dma = pltpu.SemaphoreType.DMA
    return pl.pallas_call(
        kernel,
        out_shape=jax.ShapeDtypeStruct((share, out_cols), BF16),
        in_specs=[hbm] * 10,
        out_specs=vmem,
        scratch_shapes=[
            pltpu.SMEM(lengths.shape, jnp.int32),
            pltpu.SMEM(positions.shape, jnp.int32),
            pltpu.VMEM((1, HD), F32),
            pltpu.VMEM((share, depth), BF16),
            pltpu.VMEM(w_query.shape, BF16),
            pltpu.VMEM(w_key.shape, BF16),
            pltpu.VMEM(w_value.shape, BF16),
            pltpu.VMEM(w_output.shape, BF16),
            pltpu.VMEM(keys.shape, BF16),
            pltpu.VMEM(values.shape, BF16),
            pltpu.VMEM((n_kvh, share, depth), F32),
            pltpu.VMEM((rows * GROUP, HD), F32),
            pltpu.VMEM((rows, GROUP, HD), BF16),
            pltpu.VMEM((rows, GROUP, HD), BF16),
            pltpu.VMEM((rows, 4, HD), F32),
            pltpu.VMEM((rows, 4, HD), F32),
            pltpu.VMEM((rows, GROUP, HD), BF16),
            pltpu.VMEM((ROWS_STEP * GROUP, 2 * HD), BF16),
            pltpu.VMEM((rows, GROUP, HD), BF16),
            pltpu.VMEM((rows, GROUP, HD), BF16),
            pltpu.VMEM((rows, GROUP, HD), BF16),
            pltpu.VMEM((n_kvh, share, out_cols), F32),
            pltpu.VMEM((n_kvh, share, out_cols), F32),
            dma((10,)),
            dma((7,)),
            dma((7,)),
            dma((rows // ROWS_STEP,)),
            dma((2,)),
            dma((2,)),
            dma((2,)),
            pltpu.SemaphoreType.REGULAR((1,)),
        ],
        compiler_params=pltpu.CompilerParams(
            collective_id=0, has_side_effects=True, vmem_limit_bytes=40 * 1024 * 1024
        ),
        name="decode_step",
    )(
        *(
            pltpu.with_memory_space_constraint(a, pltpu.HBM)
            for a in (
                lengths, positions, jnp.asarray(rotary_table()), inputs,
                w_query, w_key, w_value, w_output, keys, values,
            )
        )
    )


def solution(mesh):
    return jax.shard_map(
        body,
        mesh=mesh,
        in_specs=(
            P("kvh", "seq"),
            P("seq", "kvh"),
            P("seq", "kvh"),
            P("seq", "kvh"),
            P("kvh", "seq"),
            P(None, "seq", "kvh", None),
            P(None, "seq", "kvh", None),
            P(None),
            P(None),
        ),
        out_specs=P("kvh", "seq"),
        check_vma=False,
    )
```

```python
import jax
import jax.numpy as jnp
import numpy as np
from jax import lax
from jax.experimental import pallas as pl
from jax.experimental.pallas import tpu as pltpu
from jax.sharding import PartitionSpec as P

QH = 128
KVH = 8
HD = 128
GROUP = QH // KVH
MESH = pl.DeviceIdType.MESH
F32 = jnp.float32
BF16 = jnp.bfloat16
ROWS_STEP = 8
HALF = 16


def rotary_table():
    half = HD // 2
    freq = 500000.0 ** (-np.arange(half, dtype=np.float64) * 2.0 / HD)
    return np.tile(freq.astype(np.float32), 2).reshape(1, HD)


def hops(offset, sizes):
    return sum(min(d, n - d) for d, n in zip(offset, sizes))


def by_distance(sizes):
    return sorted(np.ndindex(*sizes), key=lambda o: hops(o, sizes))


SEQ_SIZES = (4, 8)
KVH_SIZES = (4, 2)
SEQ_OFFSETS = by_distance(SEQ_SIZES)
KVH_OFFSETS = by_distance(KVH_SIZES)


def peer(index, offset, sizes):
    outer, inner = sizes
    return ((index // inner + offset[0]) % outer) * inner + (index % inner + offset[1]) % inner


def kernel(
    lengths_hbm, positions_hbm, freq_hbm, inputs, wq_hbm, wk_hbm, wv_hbm, wo_hbm, key_hbm, value_hbm,
    out_ref,
    lengths, positions, freq, x_own, wq, wk, wv, wo, keys, values,
    x_all, rel, q_send, q_recv, stat_send, stat_recv, q_all, q_block,
    part_send, part_recv, heads_all, out_send, out_recv,
    load_sem, send_sem, recv_sem, group_sem, part_sem, stat_sem, heads_sem, entry_sem,
):
    seq = lax.axis_index("seq")
    kvh = lax.axis_index("kvh")
    n_seq = len(SEQ_OFFSETS)
    n_kvh = len(KVH_OFFSETS)
    rows = q_all.shape[0]
    share = x_own.shape[0]
    block = keys.shape[1]
    scale = HD ** (-0.5)
    lanes = ROWS_STEP * GROUP
    seq_peers = [peer(seq, o, SEQ_SIZES) for o in SEQ_OFFSETS]
    kvh_peers = [peer(kvh, o, KVH_SIZES) for o in KVH_OFFSETS]
    place_of = {o: p for p, o in enumerate(SEQ_OFFSETS)}
    back = [place_of[tuple(-d % n for d, n in zip(o, SEQ_SIZES))] for o in SEQ_OFFSETS]
    near = [p for p in range(n_seq - 1, 0, -1) if hops(SEQ_OFFSETS[p], SEQ_SIZES) <= 3]
    far_first = list(range(n_seq - 1, 0, -1))
    distance = [hops(o, SEQ_SIZES) for o in SEQ_OFFSETS]
    turn = (0, 1, 3, 2)
    gather_order = sorted(far_first, key=lambda p: ((1, 2, 3, 0)[back[p] // ROWS_STEP], -distance[p]))

    def load(src, dst, n):
        copy = pltpu.make_async_copy(src, dst, load_sem.at[n])
        copy.start()
        return copy

    x_load = load(inputs, x_own, 0)
    small = [load(positions_hbm, positions, 1), load(freq_hbm, freq, 2), load(lengths_hbm, lengths, 3)]
    wk_load = load(wk_hbm, wk, 4)
    wv_load = load(wv_hbm, wv, 5)
    wq_load = load(wq_hbm, wq, 6)
    key_load = load(key_hbm, keys, 7)
    value_load = load(value_hbm, values, 8)
    wo_load = load(wo_hbm, wo, 9)

    barrier = pltpu.get_barrier_semaphore()
    for p in range(n_kvh - 1, 0, -1):
        pl.semaphore_signal(barrier, inc=1, device_id={"kvh": kvh_peers[p]}, device_id_type=MESH)
    for p in near:
        pl.semaphore_signal(barrier, inc=1, device_id={"seq": seq_peers[p]}, device_id_type=MESH)
    q_block[...] = jnp.zeros_like(q_block)
    x_load.wait()
    pieces = x_own.shape[1] // HD
    x_wide = x_own[...].astype(F32)
    x_all[kvh] = jnp.concatenate(
        [x_wide[:, c * HD : (c + 1) * HD] for c in range(pieces)], axis=0
    ).astype(BF16)
    pl.semaphore_wait(barrier, len(near) + n_kvh - 1)

    def tell(step):
        for p in near:
            pl.semaphore_signal(entry_sem.at[step], inc=1, device_id={"seq": seq_peers[p]}, device_id_type=MESH)

    def send(axis, to, src, dst, phase, arrived):
        pltpu.make_async_remote_copy(
            src_ref=src, dst_ref=dst, send_sem=send_sem.at[phase], recv_sem=arrived,
            device_id={axis: to}, device_id_type=MESH,
        ).start()

    def sums_of(ref, count, phase, arrived):
        return pltpu.make_async_remote_copy(
            src_ref=ref.at[pl.ds(0, count)], dst_ref=ref.at[pl.ds(0, count)],
            send_sem=send_sem.at[phase], recv_sem=arrived,
            device_id={"kvh": kvh_peers[1]}, device_id_type=MESH,
        )

    def received(ref, count, phase):
        sums_of(ref, count, phase, recv_sem.at[phase]).wait_recv()

    def sent(ref, count, phase):
        sums_of(ref, count, phase, recv_sem.at[phase]).wait_send()

    for p in range(n_kvh - 1, 0, -1):
        send("kvh", kvh_peers[p], x_all.at[kvh], x_all.at[kvh], 0, recv_sem.at[0])
    tell(0)

    for copy in small:
        copy.wait()
    angle = positions[seq].astype(F32) * freq[...]
    cosine = jnp.cos(angle)
    sine = jnp.sin(angle)
    lane = lax.broadcasted_iota(jnp.int32, (1, HD), 1)
    sine = jnp.where(lane < HD // 2, -sine, sine)

    def rotate(t):
        return t * cosine + pltpu.roll(t, HD // 2, 1) * sine

    wk_load.wait()
    wv_load.wait()
    wq_load.wait()
    received(x_all, n_kvh - 1, 0)
    x_wide = x_all[...].astype(F32)
    x = jnp.concatenate(
        [
            jnp.concatenate([x_wide[i, c * share : (c + 1) * share] for i in range(n_kvh)], axis=0)
            for c in range(pieces)
        ],
        axis=1,
    ).astype(BF16)

    for c in range(0, GROUP, 2):
        part = jnp.dot(x, wq[:, c * HD : (c + 2) * HD], preferred_element_type=F32)
        rel[pl.ds(c, rows, stride=GROUP), :] = part[:, :HD]
        rel[pl.ds(c + 1, rows, stride=GROUP), :] = part[:, HD:]
    q_send[...] = rel[...].astype(BF16).reshape(q_send.shape)

    pl.semaphore_wait(entry_sem.at[0], len(near))
    for p in far_first:
        to = seq_peers[p]
        send("seq", to, q_send.at[to], q_recv.at[seq], 1, recv_sem.at[1])
    q_recv[seq] = q_send[seq]
    k_part = jnp.dot(x, wk[...], preferred_element_type=F32)
    v_part = jnp.dot(x, wv[...], preferred_element_type=F32)
    for r in range(rows):
        stat_send[r, 2:3, :] = k_part[r : r + 1, :]
        stat_send[r, 3:4, :] = v_part[r : r + 1, :]
    received(q_recv, n_seq - 1, 1)
    q_own = rotate(jnp.sum(q_recv[...].astype(F32), axis=0)).astype(BF16)
    q_all[seq] = q_own

    for p in gather_order:
        send("seq", seq_peers[p], q_all.at[seq], q_all.at[seq], 2, group_sem.at[back[p] // ROWS_STEP])
    sent(x_all, n_kvh - 1, 0)
    sent(q_send, n_seq - 1, 1)

    place = seq * block + lax.broadcasted_iota(jnp.int32, (GROUP, block), 1)
    lane_of = lax.broadcasted_iota(jnp.int32, (lanes, lanes), 1)
    key_load.wait()
    value_load.wait()
    groups = rows // ROWS_STEP
    for g in turn:
        here = seq_peers[g * ROWS_STEP : (g + 1) * ROWS_STEP]
        sums_of(q_all, ROWS_STEP - (g == 0), 2, group_sem.at[g]).wait_recv()
        pieces = []
        for j in range(0, ROWS_STEP, 2):
            q_block[j * GROUP : (j + 1) * GROUP, :HD] = q_all[here[j]]
            q_block[(j + 1) * GROUP : (j + 2) * GROUP, HD:] = q_all[here[j + 1]]
            k_cat = jnp.concatenate([keys[here[j]], keys[here[j + 1]]], axis=1)
            pieces.append(lax.dot_general(
                q_block[j * GROUP : (j + 2) * GROUP], k_cat, (((1,), (1,)), ((), ())), preferred_element_type=F32
            ))
        scores = jnp.concatenate(pieces, axis=0) * scale
        valid = jnp.concatenate([place < lengths[row] for row in here], axis=0)
        masked = jnp.where(valid, scores, F32(-1e30))
        block_max = jnp.max(masked, axis=1, keepdims=True)
        weights = jnp.where(valid, jnp.exp(masked - block_max), F32(0.0))
        total = jnp.sum(weights, axis=1, keepdims=True)
        turned = weights.astype(BF16)
        for j in range(0, ROWS_STEP, 2):
            v_cat = jnp.concatenate([values[here[j]], values[here[j + 1]]], axis=1)
            got = jnp.dot(
                turned[j * GROUP : (j + 2) * GROUP], v_cat, preferred_element_type=F32
            ).astype(BF16)
            part_send[here[j]] = got[:GROUP, :HD]
            part_send[here[j + 1]] = got[GROUP:, HD:]
        stats = jnp.where(lane_of == 0, block_max, total).T[:2]
        for j, row in enumerate(here):
            stat_send[row, 0:2, :] = pltpu.roll(stats, (lanes - j * GROUP) % lanes, 1)
        late = g >= groups // 2
        for p in range((g + 1) * ROWS_STEP - 1, max(g * ROWS_STEP, 1) - 1, -1):
            to = seq_peers[p]
            send("seq", to, part_send.at[to], part_recv.at[back[p]], 3, part_sem.at[back[p] // HALF])
            if late:
                send("seq", to, stat_send.at[to], stat_recv.at[back[p]], 4, stat_sem.at[back[p] // HALF])
    for p in far_first[groups // 2 * ROWS_STEP :]:
        to = seq_peers[p]
        send("seq", to, stat_send.at[to], stat_recv.at[back[p]], 4, stat_sem.at[back[p] // HALF])

    part_recv[0] = part_send[seq]
    stat_recv[0] = stat_send[seq]
    sent(q_all, n_seq - 1, 2)
    top = total = summed = None
    for wave in range(2):
        first = wave * HALF
        count = HALF - (wave == 0)
        sums_of(stat_recv, count, 4, stat_sem.at[wave]).wait_recv()
        stats = stat_recv[first : first + HALF]
        maxima = stats[:, 0, :].T[:GROUP]
        totals = stats[:, 1, :].T[:GROUP]
        k_new = jnp.sum(stats[:, 2, :], axis=0, keepdims=True) + (k_new if wave else 0.0)
        v_new = jnp.sum(stats[:, 3, :], axis=0, keepdims=True) + (v_new if wave else 0.0)
        here_top = jnp.max(maxima, axis=1, keepdims=True)
        if wave:
            k_new = rotate(k_new).astype(BF16).astype(F32)
            v_new = v_new.astype(BF16).astype(F32)
            new_score = jnp.sum(q_own.astype(F32) * k_new, axis=1, keepdims=True) * scale
            here_top = jnp.maximum(jnp.maximum(here_top, new_score), top)
            kept = jnp.exp(top - here_top)
            own = jnp.exp(new_score - here_top)
            total = total * kept + own
            summed = summed * kept + own * v_new
        top = here_top
        factor = jnp.exp(maxima - top)
        here_total = jnp.sum(factor * totals, axis=1, keepdims=True)
        total = total + here_total if wave else here_total
        sums_of(part_recv, count, 3, part_sem.at[wave]).wait_recv()
        for s in range(HALF):
            term = factor[:, s : s + 1] * part_recv[first + s].astype(F32)
            summed = term if summed is None else summed + term
    heads_all[seq] = (summed / total).astype(BF16)

    outer, inner = SEQ_SIZES
    y = seq // inner
    half = seq % inner // share

    def urgency(p):
        dy = min(SEQ_OFFSETS[p][0], outer - SEQ_OFFSETS[p][0])
        return (distance[p] < 5, dy == 2, -distance[p])

    for p in sorted(far_first, key=urgency):
        dy = SEQ_OFFSETS[p][0]
        to = seq_peers[p]
        if dy == 0:
            wave = 0
        elif dy in (1, outer - 1):
            wave = (half + to % inner // share) % 2
        else:
            wave = 1
        send("seq", to, heads_all.at[seq], heads_all.at[seq], 5, heads_sem.at[wave])
    sent(part_send, n_seq - 1, 3)
    sent(stat_send, n_seq - 1, 4)
    wo_load.wait()
    blocks = [
        [(0, 0), (0, 1), (1, 0), (outer - 1, 0)],
        [(1, 1), (outer - 1, 1), (2, 0), (2, 1)],
    ]
    cuts = out_ref.shape[1] // HD
    for wave in range(2):
        quads = [(y + dy) % outer * 2 + (half + dh) % 2 for dy, dh in blocks[wave]]
        sums_of(heads_all, HALF - (wave == 0), 5, heads_sem.at[wave]).wait_recv()
        for i, quad in enumerate(quads):
            rel[i * share * GROUP : (i + 1) * share * GROUP] = (
                heads_all[pl.ds(quad * share, share)].reshape(share * GROUP, HD).astype(F32)
            )
        heads = jnp.concatenate(
            [rel[pl.ds(h, HALF, stride=GROUP), :].astype(BF16) for h in range(GROUP)], axis=1
        )
        terms = jnp.dot(heads, wo[...], preferred_element_type=F32)
        for i, quad in enumerate(quads):
            block_of = terms[i * share : (i + 1) * share, :]
            out_send[quad] = jnp.concatenate(
                [block_of[:, c * HD : (c + 1) * HD] for c in range(cuts)], axis=0
            ).astype(BF16)
        for quad in quads:

            @pl.when(quad != kvh)
            def _():
                send("kvh", quad, out_send.at[quad], out_recv.at[kvh], 6, recv_sem.at[6])

    out_recv[kvh] = out_send[kvh]
    sent(heads_all, n_seq - 1, 5)
    received(out_recv, n_kvh - 1, 6)
    whole = jnp.sum(out_recv[...].astype(F32), axis=0)
    out_ref[...] = jnp.concatenate(
        [whole[c * share : (c + 1) * share] for c in range(cuts)], axis=1
    ).astype(out_ref.dtype)
    sent(out_send, n_kvh - 1, 6)


def body(inputs, w_query, w_key, w_value, w_output, key_cache, value_cache, lengths, positions):
    n_kvh = lax.axis_size("kvh")
    share, depth = inputs.shape
    rows, block = key_cache.shape[:2]
    out_cols = w_output.shape[1]
    keys = jnp.transpose(key_cache, (0, 2, 1, 3)).reshape(rows, block, HD)
    values = jnp.transpose(value_cache, (0, 2, 1, 3)).reshape(rows, block, HD)
    vmem = pl.BlockSpec(memory_space=pltpu.VMEM)
    hbm = pl.BlockSpec(memory_space=pltpu.HBM)
    dma = pltpu.SemaphoreType.DMA
    return pl.pallas_call(
        kernel,
        out_shape=jax.ShapeDtypeStruct((share, out_cols), BF16),
        in_specs=[hbm] * 10,
        out_specs=vmem,
        scratch_shapes=[
            pltpu.SMEM(lengths.shape, jnp.int32),
            pltpu.SMEM(positions.shape, jnp.int32),
            pltpu.VMEM((1, HD), F32),
            pltpu.VMEM((share, depth), BF16),
            pltpu.VMEM(w_query.shape, BF16),
            pltpu.VMEM(w_key.shape, BF16),
            pltpu.VMEM(w_value.shape, BF16),
            pltpu.VMEM(w_output.shape, BF16),
            pltpu.VMEM(keys.shape, BF16),
            pltpu.VMEM(values.shape, BF16),
            pltpu.VMEM((n_kvh, share * depth // HD, HD), BF16),
            pltpu.VMEM((rows * GROUP, HD), F32),
            pltpu.VMEM((rows, GROUP, HD), BF16),
            pltpu.VMEM((rows, GROUP, HD), BF16),
            pltpu.VMEM((rows, 4, HD), F32),
            pltpu.VMEM((rows, 4, HD), F32),
            pltpu.VMEM((rows, GROUP, HD), BF16),
            pltpu.VMEM((ROWS_STEP * GROUP, 2 * HD), BF16),
            pltpu.VMEM((rows, GROUP, HD), BF16),
            pltpu.VMEM((rows, GROUP, HD), BF16),
            pltpu.VMEM((rows, GROUP, HD), BF16),
            pltpu.VMEM((n_kvh, share * out_cols // HD, HD), BF16),
            pltpu.VMEM((n_kvh, share * out_cols // HD, HD), BF16),
            dma((10,)),
            dma((7,)),
            dma((7,)),
            dma((rows // ROWS_STEP,)),
            dma((2,)),
            dma((2,)),
            dma((2,)),
            pltpu.SemaphoreType.REGULAR((1,)),
        ],
        compiler_params=pltpu.CompilerParams(
            collective_id=0, has_side_effects=True, vmem_limit_bytes=40 * 1024 * 1024
        ),
        name="decode_step",
    )(
        *(
            pltpu.with_memory_space_constraint(a, pltpu.HBM)
            for a in (
                lengths, positions, jnp.asarray(rotary_table()), inputs,
                w_query, w_key, w_value, w_output, keys, values,
            )
        )
    )


def solution(mesh):
    return jax.shard_map(
        body,
        mesh=mesh,
        in_specs=(
            P("kvh", "seq"),
            P("seq", "kvh"),
            P("seq", "kvh"),
            P("seq", "kvh"),
            P("kvh", "seq"),
            P(None, "seq", "kvh", None),
            P(None, "seq", "kvh", None),
            P(None),
            P(None),
        ),
        out_specs=P("kvh", "seq"),
        check_vma=False,
    )
```
